32 devices in a mesh: groups: 2 (over x), gx: 16 (over z, y, core).
Axes of the slice: x: 2, y: 2, z: 4, core: 2. Of those that a mesh axis runs over, the one named last changes fastest.
Arguments:
- particle_state: float32 [6, 8192], P(None, ('groups', 'gx')), parts along dimension 1, may hold values from -6 to 6
- neighbours: int32 [2, 24, 8192], P(None, None, ('groups', 'gx')), parts along dimension 2, may hold values from 0 to 511
- neighbour_mask: int32 [2, 24, 8192], P(None, None, ('groups', 'gx')), parts along dimension 2, may hold values 0 or 1
- face_rows: int32 [2, 2, 4096], P(None, None, ('groups', 'gx')), parts along dimension 2, may hold values from 0 to 255
- migrants: int32 [1, 2, 1024], P(None, None, ('groups', 'gx')), parts along dimension 2, may hold values from 0 to 255
- new_order: int32 [1, 8192], P(None, ('groups', 'gx')), parts along dimension 1, may hold values from 0 to 319
- loss_weights: float32 [2, 6, 8192], P(None, None, ('groups', 'gx')), parts along dimension 2, may hold values from -6 to 6
- encoder: float32 [64, 3], replicated, may hold values from -3.5 to 3.5
- pair_weights: float32 [2, 2, 64, 64], replicated, may hold values from -0.75 to 0.75
- geometry_weights: float32 [2, 64, 4], replicated, may hold values from -3 to 3
- message_weights: float32 [2, 64, 64], replicated, may hold values from -0.75 to 0.75
- update_weights: float32 [2, 64, 128], replicated, may hold values from -0.5 to 0.5
- update_gain: float32 [2, 64], replicated, may hold values from 0.1 to 1.9
- decoder: float32 [3, 64], replicated, may hold values from -0.75 to 0.75
Outputs:
- state_grad: float32 [6, 8192], P(None, ('groups', 'gx')), parts along dimension 1
- pair_grad: float32 [4, 2, 64, 64], P('groups'), parts along dimension 0
- message_grad: float32 [4, 64, 64], P('groups'), parts along dimension 0
- update_grad: float32 [4, 64, 128], P('groups'), parts along dimension 0
The draws below stay inside these ranges and needn't reach their ends.
There are 2 independent parts, one for each index of `groups`. The reference program is written for one: setup_inputs(seed, part) draws one part's arguments, and reference() takes and returns one part's arrays. A program takes and returns all parts, laid end to end along the dimension named above; an argument that names none is the same for every part. Nothing has to cross between parts.
Inputs may be any that keep to these rules, and one draw needn't show every extreme that they name: `neighbours`: index the slab's own 256 particles, then 128 from the slab below, then 128 from the slab above. `face_rows`: local particle rows. `migrants`: local particle rows. `new_order`: index the slab's 256 particles, then 32 from below, then 32 from above.
All inputs are finite; a program needn't handle non-finite values. No bound on the sum of `neighbour_mask` on one device may be relied on, other than what follows from the above.
Results may differ from the reference program's by a relative error of at most 0.0001.
Values sent between devices are 32-bit elements; how exact they have to be, the bound alone decides.
A program may use at most 128 MiB of HBM per device.

```python
import math
import jax
import jax.numpy as jnp
from jax import lax

WIDTH = 64
NEIGHBOURS = 24
LAYERS = 2
STEPS = 2
PART_DEV = 256
HALO = 128
MIG = 32
PARTICLES = 4096
N_GX = 16


def touch_ends(entries, key, least, high):
    place = [jax.random.randint(jax.random.fold_in(key, axis), (), 0, length) for axis, length in enumerate(entries.shape)]
    longest = entries.shape.index(max(entries.shape))
    neighbour = place[:longest] + [(place[longest] + 1) % entries.shape[longest]] + place[longest + 1:]
    return entries.at[tuple(place)].set(least).at[tuple(neighbour)].set(high)


def block_scale(key, shape, cuts, smallest, largest):
    level = 1.0
    for axis_at, parts in cuts:
        heights = jax.random.uniform(jax.random.fold_in(jax.random.fold_in(key, 6), axis_at), (parts,), jnp.float32, smallest / len(cuts), largest / len(cuts))
        level = level * jnp.repeat(jnp.exp(heights), shape[axis_at] // parts).reshape((-1,) + (1,) * (len(shape) - 1 - axis_at))
    return level


def noise(own_key, shape, deviation, limit, cuts=(), dtype=jnp.bfloat16):
    entries = deviation * jax.random.normal(own_key, shape, jnp.float32)
    if cuts:
        entries = entries * block_scale(own_key, shape, cuts, -0.22, 0.18)
    return jnp.clip(entries, -limit, limit).astype(dtype)


def setup_inputs(seed: int = 0, part: int = 0) -> dict:
    arg_keys = jax.random.split(jax.random.key(seed), 15)
    part_splits = jax.random.split(jax.random.fold_in(arg_keys[14], part), 15)
    particle_state = noise(part_splits[0], (6, PARTICLES), 1.0, 6.0, ((1, 16),), jnp.float32)
    neighbours = touch_ends(jax.random.randint(part_splits[1], (STEPS, NEIGHBOURS, PARTICLES), 0, PART_DEV + 2 * HALO), jax.random.fold_in(part_splits[1], 1), 0, (PART_DEV + 2 * HALO) - 1).astype(jnp.int32)
    neighbour_mask = touch_ends((jax.random.randint(part_splits[2], (STEPS, NEIGHBOURS, PARTICLES), 0, 4) < 3).astype(jnp.int32), jax.random.fold_in(part_splits[2], 1), 0, 1)
    face_rows = touch_ends(jax.random.randint(part_splits[3], (STEPS, 2, HALO * N_GX), 0, PART_DEV), jax.random.fold_in(part_splits[3], 1), 0, PART_DEV - 1).astype(jnp.int32)
    migrants = touch_ends(jax.random.randint(part_splits[4], (STEPS - 1, 2, MIG * N_GX), 0, PART_DEV), jax.random.fold_in(part_splits[4], 1), 0, PART_DEV - 1).astype(jnp.int32)
    new_order = touch_ends(jax.random.randint(part_splits[5], (STEPS - 1, PARTICLES), 0, PART_DEV + 2 * MIG), jax.random.fold_in(part_splits[5], 1), 0, (PART_DEV + 2 * MIG) - 1).astype(jnp.int32)
    loss_weights = noise(part_splits[6], (STEPS, 6, PARTICLES), 1.0, 6.0, ((2, 16),), jnp.float32)
    encoder = noise(arg_keys[7], (WIDTH, 3), 3 ** -0.5, 3.5, (), jnp.float32)
    pair_weights = noise(arg_keys[8], (LAYERS, 2, WIDTH, WIDTH), WIDTH ** -0.5, 0.75, (), jnp.float32)
    geometry_weights = noise(arg_keys[9], (LAYERS, WIDTH, 4), 4 ** -0.5, 3.0, (), jnp.float32)
    message_weights = noise(arg_keys[10], (LAYERS, WIDTH, WIDTH), WIDTH ** -0.5, 0.75, (), jnp.float32)
    update_weights = noise(arg_keys[11], (LAYERS, WIDTH, 2 * WIDTH), (2 * WIDTH) ** -0.5, 0.5, (), jnp.float32)
    update_gain = jnp.clip(1.0 + 0.18 * jax.random.normal(arg_keys[12], (LAYERS, WIDTH), jnp.float32), 0.1, 1.9)
    decoder = noise(arg_keys[13], (3, WIDTH), WIDTH ** -0.5, 0.75, (), jnp.float32)
    return dict(particle_state=particle_state, neighbours=neighbours, neighbour_mask=neighbour_mask, face_rows=face_rows, migrants=migrants, new_order=new_order, loss_weights=loss_weights, encoder=encoder, pair_weights=pair_weights, geometry_weights=geometry_weights, message_weights=message_weights, update_weights=update_weights, update_gain=update_gain, decoder=decoder)


HIGHEST = lax.Precision.HIGHEST
TIME_STEP = 0.5
EPSILON = 1e-05

def apply_layer(places, latent, halo_part, pair_layer, message_layer, update_layer, geometry_layer, gain_layer, neighbour_rows, mask_rows):
    features = latent.shape[0]
    row_total = latent.shape[1]
    slot_total = neighbour_rows.shape[0]
    joined = jnp.concatenate([jnp.concatenate([places, latent], axis=0), halo_part], axis=1)
    projected = jnp.dot(pair_layer[1], joined[3:], precision=HIGHEST)
    flat_index = neighbour_rows.reshape(-1)
    senders = jnp.take(projected, flat_index, axis=1).reshape(features, slot_total, row_total)
    sender_places = jnp.take(joined[:3], flat_index, axis=1).reshape(3, slot_total, row_total)
    offsets = sender_places - places[:, None, :]
    distance = jnp.sqrt(lax.optimization_barrier(jnp.sum(offsets * offsets, axis=0, keepdims=True)) + 1.0)
    geometry = jnp.concatenate([offsets, distance], axis=0)
    own_part = jnp.dot(pair_layer[0], latent, precision=HIGHEST)
    pre_act = own_part[:, None, :] + senders + jnp.einsum('of,fkp->okp', geometry_layer, geometry, precision=HIGHEST)
    edge_hidden = jax.nn.silu(pre_act)
    messages = jax.nn.silu(jnp.einsum('oh,hkp->okp', message_layer, edge_hidden, precision=HIGHEST))
    collected = lax.optimization_barrier(jnp.sum(messages * mask_rows[None], axis=1)) / slot_total
    update = jnp.dot(update_layer, jnp.concatenate([latent, collected], axis=0), precision=HIGHEST)
    centred = update - lax.optimization_barrier(jnp.mean(update, axis=0, keepdims=True))
    normed = centred * lax.rsqrt(lax.optimization_barrier(jnp.mean(centred * centred, axis=0, keepdims=True)) + EPSILON)
    return latent + gain_layer[:, None] * normed

def to_blocks(array):
    shaped = array.reshape(array.shape[:-1] + (N_GX, PART_DEV))
    return jnp.moveaxis(shaped, -2, 0)

def from_blocks(array):
    moved = jnp.moveaxis(array, 0, -2)
    return moved.reshape(moved.shape[:-2] + (N_GX * PART_DEV,))

def extend(blocks, upward, downward):
    going_up = jnp.take_along_axis(blocks, upward[:, None, :], axis=2)
    going_down = jnp.take_along_axis(blocks, downward[:, None, :], axis=2)
    from_low = jnp.concatenate([jnp.zeros_like(going_up[:1]), going_up[:-1]], axis=0)
    from_high = jnp.concatenate([going_down[1:], jnp.zeros_like(going_down[:1])], axis=0)
    return jnp.concatenate([blocks, from_low, from_high], axis=2)

def reference(particle_state, neighbours, neighbour_mask, face_rows, migrants, new_order, loss_weights, encoder, pair_weights, geometry_weights, message_weights, update_weights, update_gain, decoder):
    blocked_state = to_blocks(particle_state)
    blocked_neighbours = to_blocks(neighbours)
    blocked_mask = to_blocks(neighbour_mask).astype(jnp.float32)
    blocked_loss = to_blocks(loss_weights)
    face_up = face_rows[:, 0].reshape(STEPS, N_GX, HALO)
    face_down = face_rows[:, 1].reshape(STEPS, N_GX, HALO)
    move_up = migrants[:, 0].reshape(STEPS - 1, N_GX, MIG)
    move_down = migrants[:, 1].reshape(STEPS - 1, N_GX, MIG)
    order_blocks = new_order.reshape(STEPS - 1, N_GX, PART_DEV)
    layer_blocks = jax.checkpoint(jax.vmap(apply_layer, in_axes=(0, 0, 0, None, None, None, None, None, 0, 0)))

    def total_loss(state, pair_all, message_all, update_all):
        current = state
        loss_value = jnp.float32(0.0)
        for step_index in range(STEPS):
            places = current[:, :3]
            speeds = current[:, 3:]
            latent = jnp.einsum('hc,bcp->bhp', encoder, speeds, precision=HIGHEST)
            for layer_index in range(LAYERS):
                joined = jnp.concatenate([places, latent], axis=1)
                halo_part = extend(joined, face_up[step_index], face_down[step_index])[:, :, PART_DEV:]
                latent = layer_blocks(places, latent, halo_part, pair_all[layer_index], message_all[layer_index], update_all[layer_index], geometry_weights[layer_index], update_gain[layer_index], blocked_neighbours[:, step_index], blocked_mask[:, step_index])
            acceleration = jnp.einsum('ch,bhp->bcp', decoder, latent, precision=HIGHEST)
            speeds_new = speeds + TIME_STEP * acceleration
            places_new = places + TIME_STEP * speeds_new
            advanced = jnp.concatenate([places_new, speeds_new], axis=1)
            loss_value = loss_value + jnp.sum(blocked_loss[:, step_index] * advanced)
            if step_index + 1 < STEPS:
                widened = extend(advanced, move_up[step_index], move_down[step_index])
                current = jnp.take_along_axis(widened, order_blocks[step_index][:, None, :], axis=2)
        return loss_value
    grads = jax.grad(total_loss, argnums=(0, 1, 2, 3))(blocked_state, pair_weights, message_weights, update_weights)
    factor = 1.0 / math.sqrt(N_GX * PART_DEV)
    return (from_blocks(grads[0]), grads[1] * factor, grads[2] * factor, grads[3] * factor)
```

```python
from functools import partial
import math

import jax
import jax.numpy as jnp
from jax import lax
from jax.experimental import pallas as pl
from jax.experimental.pallas import tpu as pltpu
from jax.sharding import PartitionSpec as P

HIGHEST = lax.Precision.HIGHEST
TIME_STEP = 0.5
EPSILON = 1e-05
F32 = jnp.float32
BF16 = jnp.bfloat16
GROUP = 4


def dot(a, b):
    return jnp.dot(a, b, precision=HIGHEST, preferred_element_type=F32)


def dot_nt(a, b, precision=HIGHEST):
    return lax.dot_general(
        a, b, (((1,), (1,)), ((), ())), precision=precision, preferred_element_type=F32
    )


def split(x):
    high = x.astype(BF16)
    low = (x - high.astype(F32)).astype(BF16)
    return high, low


def split_rows(x):
    high, low = split(x)
    return jnp.concatenate([high, low], axis=0)


def wide_weight(w):
    high = w.astype(BF16).astype(F32)
    return jnp.concatenate([high, high, w - high], axis=1).astype(BF16)


def hot(values, rows, start=0):
    count = lax.broadcasted_iota(jnp.int32, (rows, values.shape[1]), 0) + start
    return jnp.where(count == values, 1.0, 0.0).astype(BF16)


def kernel(
    size,
    chunk,
    state_ref,
    nb_ref,
    mask_ref,
    face_ref,
    mig_ref,
    order_ref,
    loss_ref,
    enc_ref,
    pair_ref,
    geo_ref,
    msg_ref,
    upd_ref,
    gain_ref,
    dec_ref,
    sg_ref,
    pg_ref,
    mg_ref,
    ug_ref,
    oh_ref,
    mrow_ref,
    q_ref,
    r_ref,
    act_ref,
    slope_ref,
    mslope_ref,
    faces_ref,
    pv_ref,
    sbuf,
    rbuf,
    gbuf,
    gather_buf,
    final_buf,
    send_sem,
    recv_sem,
    rs_send,
    rs_recv,
    ag_send,
    ag_recv,
):
    steps, slots, parts = nb_ref.shape
    layers, features = gain_ref.shape
    halo = face_ref.shape[2]
    moved = mig_ref.shape[2]
    joint = parts + 2 * halo
    wide = GROUP * parts
    groups = slots // GROUP
    block = 3 * features
    me = lax.axis_index("gx")

    def other(off):
        return lax.rem(me + off, size)

    barrier = pltpu.get_barrier_semaphore()

    def greet(off, carry):
        pl.semaphore_signal(
            barrier, inc=1, device_id={"gx": other(off)}, device_id_type=pl.DeviceIdType.MESH
        )
        return carry

    lax.fori_loop(1, size, greet, 0)

    for s in range(steps):

        def build(c, carry):
            for k in range(GROUP):
                row = c * GROUP + k
                lanes = slice(k * parts, (k + 1) * parts)
                oh_ref[s, c, :, lanes] = hot(nb_ref[s, pl.ds(row, 1), :], joint)
                mrow_ref[s, c, 0:1, lanes] = mask_ref[s, pl.ds(row, 1), :].astype(F32) * (
                    1.0 / slots
                )
            return carry

        lax.fori_loop(0, groups, build, 0)
        for d in range(2):
            faces_ref[s, :, d * halo : (d + 1) * halo] = hot(face_ref[s, d : d + 1, :], parts)

    pv_ref[...] = jnp.zeros_like(pv_ref)
    q_ref[...] = jnp.zeros_like(q_ref)
    sbuf[...] = jnp.zeros_like(sbuf)
    gbuf[...] = jnp.zeros_like(gbuf)

    @pl.when(me == 0)
    def _():
        rbuf[:, 0] = jnp.zeros(rbuf.shape[:1] + rbuf.shape[2:], F32)

    @pl.when(me == size - 1)
    def _():
        rbuf[:, 1] = jnp.zeros(rbuf.shape[:1] + rbuf.shape[2:], F32)

    pl.semaphore_wait(barrier, size - 1)

    def copies(x):
        up = pltpu.make_async_remote_copy(
            src_ref=sbuf.at[x, 0],
            dst_ref=rbuf.at[x, 0],
            send_sem=send_sem.at[x, 0],
            recv_sem=recv_sem.at[x, 0],
            device_id={"gx": me + 1},
            device_id_type=pl.DeviceIdType.MESH,
        )
        down = pltpu.make_async_remote_copy(
            src_ref=sbuf.at[x, 1],
            dst_ref=rbuf.at[x, 1],
            send_sem=send_sem.at[x, 1],
            recv_sem=recv_sem.at[x, 1],
            device_id={"gx": me - 1},
            device_id_type=pl.DeviceIdType.MESH,
        )
        return up, down

    def start(x):
        up, down = copies(x)
        pl.when(me < size - 1)(up.start)
        pl.when(me > 0)(down.start)

    def finish(x):
        up, down = copies(x)

        @pl.when(me > 0)
        def _():
            down.wait_send()
            up.wait_recv()

        @pl.when(me < size - 1)
        def _():
            up.wait_send()
            down.wait_recv()

    eye = jnp.where(
        lax.broadcasted_iota(jnp.int32, (features, features), 0)
        == lax.broadcasted_iota(jnp.int32, (features, features), 1),
        1.0,
        0.0,
    )
    encoder = enc_ref[...]
    dec_t = dot_nt(eye, dec_ref[...])
    gain_t = dot_nt(eye, gain_ref[...])

    def spread_rows(columns, rows):
        return sum(columns[:, c : c + 1] * rows[c] for c in range(3))

    def fold_rows(columns, array):
        return [
            jnp.sum(columns[:, c : c + 1] * array, axis=0, keepdims=True) for c in range(3)
        ]

    def tiled(x):
        return jnp.concatenate([x] * GROUP, axis=1)

    def slot_sum(x):
        return sum(x[:, k * parts : (k + 1) * parts] for k in range(GROUP))

    order = order_ref[0:1, :]
    order_own = hot(order, parts)
    low_code = jnp.where(order >= parts + moved, order - parts - moved + halo, order - parts)
    order_halo = hot(low_code, 2 * halo)
    going = [hot(mig_ref[0, d : d + 1, :], parts) for d in range(2)]

    def hot_dot(x, selector):
        rows = x.shape[0]
        pair = jnp.dot(split_rows(x), selector, preferred_element_type=F32)
        return pair[:rows] + pair[rows:]

    def hot_dot_nt(x, selector):
        rows = x.shape[0]
        pair = dot_nt(split_rows(x), selector, None)
        return pair[:rows] + pair[rows:]

    places = [state_ref[c : c + 1, :] for c in range(3)]
    speeds = [state_ref[c + 3 : c + 4, :] for c in range(3)]
    history = {}
    x_id = 0
    for s in range(steps):
        for c in range(3):
            pv_ref[s, c : c + 1, :] = places[c]
        own_places = pv_ref[s, 0:8]
        latent = spread_rows(encoder, speeds)
        for l in range(layers):
            geo = geo_ref[l]
            table = dot(pair_ref[l, 1], latent) + spread_rows(geo, places)
            first = l == 0
            leaving = jnp.concatenate([table, own_places], axis=0) if first else table
            sent = hot_dot(leaving, faces_ref[s])
            count = leaving.shape[0]
            sbuf[x_id, 0, :count] = sent[:, :halo]
            sbuf[x_id, 1, :count] = sent[:, halo:]
            start(x_id)
            own = dot(pair_ref[l, 0], latent) - spread_rows(geo, places)
            base_update = dot(upd_ref[l, :, :features], latent)
            weight = wide_weight(msg_ref[l])
            own_wide = tiled(own)
            places_wide = tiled(own_places)
            geo_r = geo[:, 3:4]
            finish(x_id)
            full = jnp.concatenate(
                [table, rbuf[x_id, 0, :features], rbuf[x_id, 1, :features]], axis=1
            )
            pieces = split_rows(full)
            if first:
                spots = jnp.concatenate(
                    [own_places, rbuf[x_id, 0, features:], rbuf[x_id, 1, features:]], axis=1
                )
                spots_high = spots.astype(BF16).astype(F32)
                spot_pieces = jnp.concatenate([spots_high, spots - spots_high], axis=0)
                pieces = jnp.concatenate([pieces, spot_pieces.astype(BF16)], axis=0)
            x_id += 1

            def edges(c, total):
                taken = jnp.dot(pieces, oh_ref[s, c], preferred_element_type=F32)
                senders = taken[:features] + taken[features : 2 * features]
                if first:
                    at = 2 * features
                    offsets = taken[at : at + 8] + taken[at + 8 : at + 16] - places_wide
                    squared = jnp.sum(offsets * offsets, axis=0, keepdims=True) + 1.0
                    distance = jnp.sqrt(squared)
                    r_ref[s, c, 0:1, :] = distance
                    q_ref[s, c] = offsets / distance
                else:
                    distance = r_ref[s, c, 0:1, :]
                pre = own_wide + senders + geo_r * distance
                gate = 0.5 * jnp.tanh(0.5 * pre) + 0.5
                hidden = pre * gate
                slope_ref[s, l, c] = gate + hidden - hidden * gate
                both = split_rows(hidden)
                act_ref[s, l, c] = both
                pre2 = jnp.dot(
                    weight,
                    jnp.concatenate([both, both[:features]], axis=0),
                    preferred_element_type=F32,
                )
                gate2 = 0.5 * jnp.tanh(0.5 * pre2) + 0.5
                message = pre2 * gate2
                scale = mrow_ref[s, c, 0:1, :]
                mslope_ref[s, l, c] = (gate2 + message - message * gate2) * scale
                return total + slot_sum(message * scale)

            collected = lax.fori_loop(0, groups, edges, jnp.zeros((features, parts), F32))
            update = base_update + dot(upd_ref[l, :, features:], collected)
            centred = update - jnp.mean(update, axis=0, keepdims=True)
            spread = lax.rsqrt(jnp.mean(centred * centred, axis=0, keepdims=True) + EPSILON)
            normed = centred * spread
            history[s, l] = (latent, collected, normed, spread)
            latent = latent + gain_t[:, l : l + 1] * normed
        gained = fold_rows(dec_t, latent)
        speeds = [speeds[c] + TIME_STEP * gained[c] for c in range(3)]
        places = [places[c] + TIME_STEP * speeds[c] for c in range(3)]
        if s + 1 < steps:
            for c in range(3):
                pv_ref[s, 8 + c : 9 + c, :] = places[c]
                pv_ref[s, 16 + c : 17 + c, :] = speeds[c]
            advanced = pv_ref[s, 8:24]
            for d in range(2):
                sbuf[x_id, d, :16, :moved] = hot_dot(advanced, going[d])
            start(x_id)
            kept = hot_dot(advanced, order_own)
            finish(x_id)
            arrived = jnp.concatenate([rbuf[x_id, 0, :16], rbuf[x_id, 1, :16]], axis=1)
            pv_ref[s, 8:24] = kept + hot_dot(arrived, order_halo)
            x_id += 1
            places = [pv_ref[s, 8 + c : 9 + c, :] for c in range(3)]
            speeds = [pv_ref[s, 16 + c : 17 + c, :] for c in range(3)]

    carried = [None] * 6
    for s in reversed(range(steps)):
        grad_out = [loss_ref[s, c : c + 1, :] for c in range(6)]
        if carried[0] is not None:
            grad_out = [a + b for a, b in zip(grad_out, carried)]
        grad_places = grad_out[:3]
        grad_speeds = [grad_out[3 + c] + TIME_STEP * grad_out[c] for c in range(3)]
        grad_latent = spread_rows(dec_t, [TIME_STEP * g for g in grad_speeds])
        far_total = jnp.zeros((8, joint), F32)
        near_total = jnp.zeros((8, parts), F32)
        for l in reversed(range(layers)):
            latent, collected, normed, spread = history[s, l]
            geo = geo_ref[l]
            geo_r = geo[:, 3:4]
            g_norm = gain_t[:, l : l + 1] * grad_latent
            g_update = spread * (
                g_norm
                - jnp.mean(g_norm, axis=0, keepdims=True)
                - normed * jnp.mean(g_norm * normed, axis=0, keepdims=True)
            )
            upd_collected_t = upd_ref[l, :, features:].T
            g_wide = tiled(dot(upd_collected_t, g_update))
            weight_t = wide_weight(msg_ref[l].T)

            def back(c, carry):
                spread_sum, own_sum, near_sum, weight_sum = carry
                g_pre2 = g_wide * mslope_ref[s, l, c]
                both = split_rows(g_pre2)
                weight_sum = weight_sum + dot_nt(both, act_ref[s, l, c], None)
                g_hidden = jnp.dot(
                    weight_t,
                    jnp.concatenate([both, both[:features]], axis=0),
                    preferred_element_type=F32,
                )
                g_pre = g_hidden * slope_ref[s, l, c]
                g_distance = jnp.sum(geo_r * g_pre, axis=0, keepdims=True)
                g_offset = q_ref[s, c] * g_distance
                offset_high = g_offset.astype(BF16).astype(F32)
                offset_pieces = jnp.concatenate([offset_high, g_offset - offset_high], axis=0)
                pieces = jnp.concatenate([split_rows(g_pre), offset_pieces.astype(BF16)], axis=0)
                spread_sum = spread_sum + dot_nt(pieces, oh_ref[s, c], None)
                return (
                    spread_sum,
                    own_sum + slot_sum(g_pre),
                    near_sum + slot_sum(g_offset),
                    weight_sum,
                )

            spread_sum, own_sum, near_sum, weight_sum = lax.fori_loop(
                0,
                groups,
                back,
                (
                    jnp.zeros((2 * features + 16, joint), F32),
                    jnp.zeros((features, parts), F32),
                    jnp.zeros((8, parts), F32),
                    jnp.zeros((2 * features, 2 * features), F32),
                ),
            )
            g_table = spread_sum[:features] + spread_sum[features : 2 * features]
            at = 2 * features
            far_total = far_total + spread_sum[at : at + 8] + spread_sum[at + 8 : at + 16]
            near_total = near_total + near_sum
            sbuf[x_id, 1, :features] = g_table[:, parts : parts + halo]
            sbuf[x_id, 0, :features] = g_table[:, parts + halo :]
            if l == 0:
                sbuf[x_id, 1, features:] = far_total[:, parts : parts + halo]
                sbuf[x_id, 0, features:] = far_total[:, parts + halo :]
            start(x_id)
            base = l * block
            gbuf[base + features : base + 2 * features, :] += dot_nt(
                g_update, jnp.concatenate([latent, collected], axis=0)
            )
            gbuf[base + 2 * features : base + block, :features] += (
                weight_sum[:features, :features]
                + weight_sum[features:, :features]
                + weight_sum[:features, features:]
                + weight_sum[features:, features:]
            )
            grad_latent = (
                grad_latent
                + dot(upd_ref[l, :, :features].T, g_update)
                + dot(pair_ref[l, 0].T, own_sum)
            )
            finish(x_id)
            returned = jnp.concatenate([rbuf[x_id, 1], rbuf[x_id, 0]], axis=1)
            if l > 0:
                returned = returned[:features]
            x_id += 1
            settled = hot_dot_nt(returned, faces_ref[s])
            g_table = g_table[:, :parts] + settled[:features]
            grad_latent = grad_latent + dot(pair_ref[l, 1].T, g_table)
            grad_places = [
                a + b for a, b in zip(grad_places, fold_rows(geo, g_table - own_sum))
            ]
            if l == 0:
                near = far_total[:, :parts] + settled[features:] - near_total
                grad_places = [grad_places[c] + near[c : c + 1] for c in range(3)]
            gbuf[base : base + features, :] += jnp.concatenate(
                [dot_nt(own_sum, latent), dot_nt(g_table, latent)], axis=1
            )
        grad_speeds = [
            a + b for a, b in zip(grad_speeds, fold_rows(encoder, grad_latent))
        ]
        if s > 0:
            for c in range(3):
                pv_ref[s, 8 + c : 9 + c, :] = grad_places[c]
                pv_ref[s, 16 + c : 17 + c, :] = grad_speeds[c]
            current = pv_ref[s, 8:24]
            handed = hot_dot_nt(current, order_halo)
            sbuf[x_id, 1, :16] = handed[:, :halo]
            sbuf[x_id, 0, :16] = handed[:, halo:]
            start(x_id)
            kept = hot_dot_nt(current, order_own)
            finish(x_id)
            pv_ref[s, 8:24] = (
                kept
                + hot_dot_nt(rbuf[x_id, 1, :16, :moved], going[0])
                + hot_dot_nt(rbuf[x_id, 0, :16, :moved], going[1])
            )
            x_id += 1
            carried = [pv_ref[s, 8 + c : 9 + c, :] for c in range(3)]
            carried += [pv_ref[s, 16 + c : 17 + c, :] for c in range(3)]
        else:
            for c in range(3):
                sg_ref[c : c + 1, :] = grad_places[c]
                sg_ref[3 + c : 4 + c, :] = grad_speeds[c]

    def rows_of(index):
        return pl.ds(pl.multiple_of(index * chunk, 8), chunk)

    def scatter_copy(off):
        return pltpu.make_async_remote_copy(
            src_ref=gbuf.at[rows_of(other(off))],
            dst_ref=gather_buf.at[off],
            send_sem=rs_send.at[off],
            recv_sem=rs_recv.at[off],
            device_id={"gx": other(off)},
            device_id_type=pl.DeviceIdType.MESH,
        )

    def gather_copy(off):
        return pltpu.make_async_remote_copy(
            src_ref=final_buf.at[rows_of(me)],
            dst_ref=final_buf.at[rows_of(me)],
            send_sem=ag_send.at[off],
            recv_sem=ag_recv.at[off],
            device_id={"gx": other(off)},
            device_id_type=pl.DeviceIdType.MESH,
        )

    def each(act):
        def body(off, carry):
            act(off)
            return carry

        lax.fori_loop(1, size, body, 0)

    each(lambda off: scatter_copy(off).start())

    def add(off, total):
        scatter_copy(off).wait_recv()
        return total + gather_buf[off]

    total = lax.fori_loop(1, size, add, gbuf[rows_of(me), :])
    final_buf[rows_of(me), :] = total * (1.0 / math.sqrt(parts * size))
    each(lambda off: gather_copy(off).start())

    def drain(off):
        scatter_copy(off).wait_send()
        gather_copy(off).wait_send()
        source = lax.rem(me - off + size, size)
        pltpu.make_async_remote_copy(
            src_ref=final_buf.at[rows_of(source)],
            dst_ref=final_buf.at[rows_of(source)],
            send_sem=ag_send.at[off],
            recv_sem=ag_recv.at[off],
            device_id={"gx": other(off)},
            device_id_type=pl.DeviceIdType.MESH,
        ).wait_recv()

    each(drain)
    for l in range(layers):
        base = l * block
        pg_ref[l, 0] = final_buf[base : base + features, :features]
        pg_ref[l, 1] = final_buf[base : base + features, features:]
        ug_ref[l] = final_buf[base + features : base + 2 * features, :]
        mg_ref[l] = final_buf[base + 2 * features : base + block, :features]


def local(size, *args):
    state, nb, _, face, mig = args[:5]
    pair, msg, upd = args[8], args[10], args[11]
    steps, slots, parts = nb.shape
    layers, features = msg.shape[:2]
    halo = face.shape[2]
    joint = parts + 2 * halo
    groups = slots // GROUP
    wide = GROUP * parts
    trades = 2 * steps * layers + 2 * (steps - 1)
    tiles = layers * 3 * features // 8
    chunk = -(-tiles // size) * 8
    rows = chunk * size
    vmem = pl.BlockSpec(memory_space=pltpu.VMEM)
    return pl.pallas_call(
        partial(kernel, size, chunk),
        out_shape=tuple(
            jax.ShapeDtypeStruct(a.shape, F32) for a in (state, pair, msg, upd)
        ),
        in_specs=[vmem] * len(args),
        out_specs=(vmem,) * 4,
        scratch_shapes=[
            pltpu.VMEM((steps, groups, joint, wide), BF16),
            pltpu.VMEM((steps, groups, 8, wide), F32),
            pltpu.VMEM((steps, groups, 8, wide), F32),
            pltpu.VMEM((steps, groups, 8, wide), F32),
            pltpu.VMEM((steps, layers, groups, 2 * features, wide), BF16),
            pltpu.VMEM((steps, layers, groups, features, wide), F32),
            pltpu.VMEM((steps, layers, groups, features, wide), F32),
            pltpu.VMEM((steps, parts, 2 * halo), BF16),
            pltpu.VMEM((steps, 24, parts), F32),
            pltpu.VMEM((trades, 2, features + 8, halo), F32),
            pltpu.VMEM((trades, 2, features + 8, halo), F32),
            pltpu.VMEM((rows, 128), F32),
            pltpu.VMEM((size, chunk, 128), F32),
            pltpu.VMEM((rows, 128), F32),
            pltpu.SemaphoreType.DMA((trades, 2)),
            pltpu.SemaphoreType.DMA((trades, 2)),
            pltpu.SemaphoreType.DMA((size,)),
            pltpu.SemaphoreType.DMA((size,)),
            pltpu.SemaphoreType.DMA((size,)),
            pltpu.SemaphoreType.DMA((size,)),
        ],
        compiler_params=pltpu.CompilerParams(
            collective_id=0, has_side_effects=True, vmem_limit_bytes=56 * 1024 * 1024
        ),
    )(*args)


def solution(mesh):
    block = ("groups", "gx")
    in_specs = (
        P(None, block),
        P(None, None, block),
        P(None, None, block),
        P(None, None, block),
        P(None, None, block),
        P(None, block),
        P(None, None, block),
    ) + (P(),) * 7
    out_specs = (
        P(None, block),
        P("groups", None, None, None),
        P("groups", None, None),
        P("groups", None, None),
    )
    return jax.shard_map(
        partial(local, mesh.shape["gx"]),
        mesh=mesh,
        in_specs=in_specs,
        out_specs=out_specs,
        check_vma=False,
    )
```

```python
from functools import partial
import math

import jax
import jax.numpy as jnp
from jax import lax
from jax.experimental import pallas as pl
from jax.experimental.pallas import tpu as pltpu
from jax.sharding import PartitionSpec as P

HIGHEST = lax.Precision.HIGHEST
TIME_STEP = 0.5
EPSILON = 1e-05
F32 = jnp.float32
BF16 = jnp.bfloat16
GROUP = 12


def dot(a, b):
    return jnp.dot(a, b, precision=HIGHEST, preferred_element_type=F32)


def dot_nt(a, b, precision=HIGHEST):
    return lax.dot_general(
        a, b, (((1,), (1,)), ((), ())), precision=precision, preferred_element_type=F32
    )


def split(x):
    high = x.astype(BF16)
    low = (x - high.astype(F32)).astype(BF16)
    return high, low


def split_rows(x):
    high, low = split(x)
    return jnp.concatenate([high, low], axis=0)


def wide_weight(w):
    high = w.astype(BF16).astype(F32)
    return jnp.concatenate([high, high, w - high], axis=1).astype(BF16)


def hot(values, rows, start=0):
    count = lax.broadcasted_iota(jnp.int32, (rows, values.shape[1]), 0) + start
    return jnp.where(count == values, 1.0, 0.0).astype(BF16)


def kernel(
    size,
    chunk,
    state_ref,
    nb_ref,
    mask_ref,
    face_ref,
    mig_ref,
    order_ref,
    loss_ref,
    enc_ref,
    pair_ref,
    geo_ref,
    msg_ref,
    upd_ref,
    gain_ref,
    dec_ref,
    sg_ref,
    packed_ref,
    oh_ref,
    mrow_ref,
    q_ref,
    r_ref,
    act_ref,
    slope_ref,
    mslope_ref,
    piece_ref,
    message_ref,
    faces_ref,
    pv_ref,
    sbuf,
    rbuf,
    gbuf,
    gather_buf,
    final_buf,
    send_sem,
    recv_sem,
    rs_send,
    rs_recv,
    ag_send,
    ag_recv,
):
    steps, slots, parts = nb_ref.shape
    layers, features = gain_ref.shape
    halo = face_ref.shape[2]
    moved = mig_ref.shape[2]
    joint = parts + 2 * halo
    wide = GROUP * parts
    groups = slots // GROUP
    block = 3 * features
    me = lax.axis_index("gx")

    def other(off):
        return lax.rem(me + off, size)

    barrier = pltpu.get_barrier_semaphore()

    def greet(off, carry):
        pl.semaphore_signal(
            barrier, inc=1, device_id={"gx": other(off)}, device_id_type=pl.DeviceIdType.MESH
        )
        return carry

    lax.fori_loop(1, size, greet, 0)

    for s in range(steps):

        def build(c, carry):
            for k in range(GROUP):
                row = c * GROUP + k
                lanes = slice(k * parts, (k + 1) * parts)
                oh_ref[s, c, :, lanes] = hot(nb_ref[s, pl.ds(row, 1), :], joint)
                mrow_ref[s, c, 0:1, lanes] = mask_ref[s, pl.ds(row, 1), :].astype(F32) * (
                    1.0 / slots
                )
            return carry

        lax.fori_loop(0, groups, build, 0)
        for d in range(2):
            faces_ref[s, :, d * halo : (d + 1) * halo] = hot(face_ref[s, d : d + 1, :], parts)

    pv_ref[...] = jnp.zeros_like(pv_ref)
    q_ref[...] = jnp.zeros_like(q_ref)
    sbuf[...] = jnp.zeros_like(sbuf)
    gbuf[...] = jnp.zeros_like(gbuf)

    @pl.when(me == 0)
    def _():
        rbuf[:, 0] = jnp.zeros(rbuf.shape[:1] + rbuf.shape[2:], F32)

    @pl.when(me == size - 1)
    def _():
        rbuf[:, 1] = jnp.zeros(rbuf.shape[:1] + rbuf.shape[2:], F32)

    pl.semaphore_wait(barrier, size - 1)

    def copies(x):
        up = pltpu.make_async_remote_copy(
            src_ref=sbuf.at[x, 0],
            dst_ref=rbuf.at[x, 0],
            send_sem=send_sem.at[x, 0],
            recv_sem=recv_sem.at[x, 0],
            device_id={"gx": me + 1},
            device_id_type=pl.DeviceIdType.MESH,
        )
        down = pltpu.make_async_remote_copy(
            src_ref=sbuf.at[x, 1],
            dst_ref=rbuf.at[x, 1],
            send_sem=send_sem.at[x, 1],
            recv_sem=recv_sem.at[x, 1],
            device_id={"gx": me - 1},
            device_id_type=pl.DeviceIdType.MESH,
        )
        return up, down

    def start(x):
        up, down = copies(x)
        pl.when(me < size - 1)(up.start)
        pl.when(me > 0)(down.start)

    def finish(x):
        up, down = copies(x)

        @pl.when(me > 0)
        def _():
            down.wait_send()
            up.wait_recv()

        @pl.when(me < size - 1)
        def _():
            up.wait_send()
            down.wait_recv()

    eye = jnp.where(
        lax.broadcasted_iota(jnp.int32, (features, features), 0)
        == lax.broadcasted_iota(jnp.int32, (features, features), 1),
        1.0,
        0.0,
    )

    def turn(rows):
        return dot_nt(eye, rows)

    encoder = turn(enc_ref[...])
    geometry = [turn(geo_ref[l]) for l in range(layers)]
    dec_t = turn(dec_ref[...])
    gain_t = turn(gain_ref[...])

    def spread_rows(columns, rows):
        return sum(columns[:, c : c + 1] * rows[c] for c in range(3))

    def fold_rows(columns, array):
        return [
            jnp.sum(columns[:, c : c + 1] * array, axis=0, keepdims=True) for c in range(3)
        ]

    def tiled(x):
        return jnp.concatenate([x] * GROUP, axis=1)

    def slot_sum(x):
        return sum(x[:, k * parts : (k + 1) * parts] for k in range(GROUP))

    order = order_ref[0:1, :]
    order_own = hot(order, parts)
    low_code = jnp.where(order >= parts + moved, order - parts - moved + halo, order - parts)
    order_halo = hot(low_code, 2 * halo)
    going = [hot(mig_ref[0, d : d + 1, :], parts) for d in range(2)]

    def hot_dot(x, selector):
        rows = x.shape[0]
        pair = jnp.dot(split_rows(x), selector, preferred_element_type=F32)
        return pair[:rows] + pair[rows:]

    def hot_dot_nt(x, selector):
        rows = x.shape[0]
        pair = dot_nt(split_rows(x), selector, None)
        return pair[:rows] + pair[rows:]

    places = [state_ref[c : c + 1, :] for c in range(3)]
    speeds = [state_ref[c + 3 : c + 4, :] for c in range(3)]
    history = {}
    x_id = 0
    for s in range(steps):
        for c in range(3):
            pv_ref[s, c : c + 1, :] = places[c]
        own_places = pv_ref[s, 0:8]
        latent = spread_rows(encoder, speeds)
        for l in range(layers):
            geo = geometry[l]
            table = dot(pair_ref[l, 1], latent) + spread_rows(geo, places)
            first = l == 0
            leaving = jnp.concatenate([table, own_places], axis=0) if first else table
            sent = hot_dot(leaving, faces_ref[s])
            count = leaving.shape[0]
            sbuf[x_id, 0, :count] = sent[:, :halo]
            sbuf[x_id, 1, :count] = sent[:, halo:]
            start(x_id)
            own = dot(pair_ref[l, 0], latent) - spread_rows(geo, places)
            base_update = dot(upd_ref[l, :, :features], latent)
            weight = wide_weight(msg_ref[l])
            own_wide = tiled(own)
            places_wide = tiled(own_places)
            geo_r = geo[:, 3:4]

            def cut(values, spots):
                pieces = split_rows(values)
                if spots is None:
                    return pieces
                high = spots.astype(BF16).astype(F32)
                rest = jnp.concatenate([high, spots - high], axis=0)
                return jnp.concatenate([pieces, rest.astype(BF16)], axis=0)

            def merge(taken):
                at = 2 * features
                values = taken[:features] + taken[features:at]
                return values, (taken[at : at + 8] + taken[at + 8 : at + 16] if first else None)

            near_pieces = cut(table, own_places if first else None)

            def near_edges(c, carry):
                senders, offsets = merge(
                    jnp.dot(near_pieces, oh_ref[s, c, :parts], preferred_element_type=F32)
                )
                slope_ref[s, l, c] = own_wide + senders
                if first:
                    q_ref[s, c] = offsets - places_wide
                return carry

            lax.fori_loop(0, groups, near_edges, 0)
            finish(x_id)
            arrived = jnp.concatenate([rbuf[x_id, 0], rbuf[x_id, 1]], axis=1)
            far_pieces = cut(arrived[:features], arrived[features:] if first else None)
            x_id += 1

            def edges(c, total):
                senders, offsets = merge(
                    jnp.dot(far_pieces, oh_ref[s, c, parts:], preferred_element_type=F32)
                )
                if first:
                    offsets = offsets + q_ref[s, c]
                    squared = jnp.sum(offsets * offsets, axis=0, keepdims=True) + 1.0
                    distance = jnp.sqrt(squared)
                    r_ref[s, c, 0:1, :] = distance
                    q_ref[s, c] = offsets / distance
                else:
                    distance = r_ref[s, c, 0:1, :]
                pre = slope_ref[s, l, c] + senders + geo_r * distance
                gate = 0.5 * jnp.tanh(0.5 * pre) + 0.5
                hidden = pre * gate
                slope_ref[s, l, c] = gate + hidden - hidden * gate
                both = split_rows(hidden)
                act_ref[s, l, c] = both
                pre2 = jnp.dot(
                    weight,
                    jnp.concatenate([both, both[:features]], axis=0),
                    preferred_element_type=F32,
                )
                gate2 = 0.5 * jnp.tanh(0.5 * pre2) + 0.5
                message = pre2 * gate2
                scale = mrow_ref[s, c, 0:1, :]
                mslope_ref[s, l, c] = (gate2 + message - message * gate2) * scale
                return total + slot_sum(message * scale)

            collected = lax.fori_loop(0, groups, edges, jnp.zeros((features, parts), F32))
            update = base_update + dot(upd_ref[l, :, features:], collected)
            centred = update - jnp.mean(update, axis=0, keepdims=True)
            spread = lax.rsqrt(jnp.mean(centred * centred, axis=0, keepdims=True) + EPSILON)
            normed = centred * spread
            history[s, l] = (latent, collected, normed, spread)
            latent = latent + gain_t[:, l : l + 1] * normed
        gained = fold_rows(dec_t, latent)
        speeds = [speeds[c] + TIME_STEP * gained[c] for c in range(3)]
        places = [places[c] + TIME_STEP * speeds[c] for c in range(3)]
        if s + 1 < steps:
            for c in range(3):
                pv_ref[s, 8 + c : 9 + c, :] = places[c]
                pv_ref[s, 16 + c : 17 + c, :] = speeds[c]
            advanced = pv_ref[s, 8:24]
            for d in range(2):
                sbuf[x_id, d, :16, :moved] = hot_dot(advanced, going[d])
            start(x_id)
            kept = hot_dot(advanced, order_own)
            finish(x_id)
            arrived = jnp.concatenate([rbuf[x_id, 0, :16], rbuf[x_id, 1, :16]], axis=1)
            pv_ref[s, 8:24] = kept + hot_dot(arrived, order_halo)
            x_id += 1
            places = [pv_ref[s, 8 + c : 9 + c, :] for c in range(3)]
            speeds = [pv_ref[s, 16 + c : 17 + c, :] for c in range(3)]

    carried = [None] * 6
    for s in reversed(range(steps)):
        grad_out = [loss_ref[c, s : s + 1, :] for c in range(6)]
        if carried[0] is not None:
            grad_out = [a + b for a, b in zip(grad_out, carried)]
        grad_places = grad_out[:3]
        grad_speeds = [grad_out[3 + c] + TIME_STEP * grad_out[c] for c in range(3)]
        grad_latent = spread_rows(dec_t, [TIME_STEP * g for g in grad_speeds])
        far_total = jnp.zeros((8, 2 * halo), F32)
        near_total = jnp.zeros((8, parts), F32)
        for l in reversed(range(layers)):
            latent, collected, normed, spread = history[s, l]
            geo = geometry[l]
            geo_r = geo[:, 3:4]
            g_norm = gain_t[:, l : l + 1] * grad_latent
            g_update = spread * (
                g_norm
                - jnp.mean(g_norm, axis=0, keepdims=True)
                - normed * jnp.mean(g_norm * normed, axis=0, keepdims=True)
            )
            upd_collected_t = upd_ref[l, :, features:].T
            g_wide = tiled(dot(upd_collected_t, g_update))
            weight_t = wide_weight(msg_ref[l].T)

            def back(c, carry):
                spread_sum, own_sum, near_sum = carry
                g_pre2 = g_wide * mslope_ref[s, l, c]
                both = split_rows(g_pre2)
                message_ref[c] = both
                g_hidden = jnp.dot(
                    weight_t,
                    jnp.concatenate([both, both[:features]], axis=0),
                    preferred_element_type=F32,
                )
                g_pre = g_hidden * slope_ref[s, l, c]
                g_distance = jnp.sum(geo_r * g_pre, axis=0, keepdims=True)
                g_offset = q_ref[s, c] * g_distance
                offset_high = g_offset.astype(BF16).astype(F32)
                offset_pieces = jnp.concatenate([offset_high, g_offset - offset_high], axis=0)
                pieces = jnp.concatenate([split_rows(g_pre), offset_pieces.astype(BF16)], axis=0)
                piece_ref[c] = pieces
                spread_sum = spread_sum + dot_nt(pieces, oh_ref[s, c, parts:], None)
                return (
                    spread_sum,
                    own_sum + slot_sum(g_pre),
                    near_sum + slot_sum(g_offset),
                )

            spread_sum, own_sum, near_sum = lax.fori_loop(
                0,
                groups,
                back,
                (
                    jnp.zeros((2 * features + 16, 2 * halo), F32),
                    jnp.zeros((features, parts), F32),
                    jnp.zeros((8, parts), F32),
                ),
            )
            at = 2 * features
            g_far = spread_sum[:features] + spread_sum[features:at]
            far_total = far_total + spread_sum[at : at + 8] + spread_sum[at + 8 : at + 16]
            sbuf[x_id, 1, :features] = g_far[:, :halo]
            sbuf[x_id, 0, :features] = g_far[:, halo:]
            if l == 0:
                sbuf[x_id, 1, features:] = far_total[:, :halo]
                sbuf[x_id, 0, features:] = far_total[:, halo:]
            start(x_id)

            def back_own(c, carry):
                spread_sum, weight_sum = carry
                return (
                    spread_sum + dot_nt(piece_ref[c], oh_ref[s, c, :parts], None),
                    weight_sum + dot_nt(message_ref[c], act_ref[s, l, c], None),
                )

            spread_sum, weight_sum = lax.fori_loop(
                0,
                groups,
                back_own,
                (
                    jnp.zeros((2 * features + 16, parts), F32),
                    jnp.zeros((2 * features, 2 * features), F32),
                ),
            )
            g_table = spread_sum[:features] + spread_sum[features:at]
            near_total = near_total + spread_sum[at : at + 8] + spread_sum[at + 8 : at + 16]
            near_total = near_total - near_sum
            base = l * block
            gbuf[base + features : base + 2 * features, :] += dot_nt(
                g_update, jnp.concatenate([latent, collected], axis=0)
            )
            gbuf[base + 2 * features : base + block, :features] += (
                weight_sum[:features, :features]
                + weight_sum[features:, :features]
                + weight_sum[:features, features:]
                + weight_sum[features:, features:]
            )
            grad_latent = (
                grad_latent
                + dot(upd_ref[l, :, :features].T, g_update)
                + dot(pair_ref[l, 0].T, own_sum)
            )
            finish(x_id)
            returned = jnp.concatenate([rbuf[x_id, 1], rbuf[x_id, 0]], axis=1)
            if l > 0:
                returned = returned[:features]
            x_id += 1
            settled = hot_dot_nt(returned, faces_ref[s])
            g_table = g_table + settled[:features]
            grad_latent = grad_latent + dot(pair_ref[l, 1].T, g_table)
            grad_places = [
                a + b for a, b in zip(grad_places, fold_rows(geo, g_table - own_sum))
            ]
            if l == 0:
                near = near_total + settled[features:]
                grad_places = [grad_places[c] + near[c : c + 1] for c in range(3)]
            gbuf[base : base + features, :] += jnp.concatenate(
                [dot_nt(own_sum, latent), dot_nt(g_table, latent)], axis=1
            )
        grad_speeds = [
            a + b for a, b in zip(grad_speeds, fold_rows(encoder, grad_latent))
        ]
        if s > 0:
            for c in range(3):
                pv_ref[s, 8 + c : 9 + c, :] = grad_places[c]
                pv_ref[s, 16 + c : 17 + c, :] = grad_speeds[c]
            current = pv_ref[s, 8:24]
            handed = hot_dot_nt(current, order_halo)
            sbuf[x_id, 1, :16] = handed[:, :halo]
            sbuf[x_id, 0, :16] = handed[:, halo:]
            start(x_id)
            kept = hot_dot_nt(current, order_own)
            finish(x_id)
            pv_ref[s, 8:24] = (
                kept
                + hot_dot_nt(rbuf[x_id, 1, :16, :moved], going[0])
                + hot_dot_nt(rbuf[x_id, 0, :16, :moved], going[1])
            )
            x_id += 1
            carried = [pv_ref[s, 8 + c : 9 + c, :] for c in range(3)]
            carried += [pv_ref[s, 16 + c : 17 + c, :] for c in range(3)]
        else:
            for c in range(3):
                sg_ref[c : c + 1, :] = grad_places[c]
                sg_ref[3 + c : 4 + c, :] = grad_speeds[c]

    def rows_of(index):
        return pl.ds(pl.multiple_of(index * chunk, 8), chunk)

    def scatter_copy(off):
        return pltpu.make_async_remote_copy(
            src_ref=gbuf.at[rows_of(other(off))],
            dst_ref=gather_buf.at[off],
            send_sem=rs_send.at[off],
            recv_sem=rs_recv.at[off],
            device_id={"gx": other(off)},
            device_id_type=pl.DeviceIdType.MESH,
        )

    def gather_copy(off):
        return pltpu.make_async_remote_copy(
            src_ref=final_buf.at[rows_of(me)],
            dst_ref=final_buf.at[rows_of(me)],
            send_sem=ag_send.at[off],
            recv_sem=ag_recv.at[off],
            device_id={"gx": other(off)},
            device_id_type=pl.DeviceIdType.MESH,
        )

    def each(act):
        def body(off, carry):
            act(off)
            return carry

        lax.fori_loop(1, size, body, 0)

    each(lambda off: scatter_copy(off).start())

    def add(off, total):
        scatter_copy(off).wait_recv()
        return total + gather_buf[off]

    total = lax.fori_loop(1, size, add, gbuf[rows_of(me), :])
    final_buf[rows_of(me), :] = total * (1.0 / math.sqrt(parts * size))
    each(lambda off: gather_copy(off).start())

    def drain(off):
        scatter_copy(off).wait_send()
        gather_copy(off).wait_send()
        source = lax.rem(me - off + size, size)
        pltpu.make_async_remote_copy(
            src_ref=final_buf.at[rows_of(source)],
            dst_ref=final_buf.at[rows_of(source)],
            send_sem=ag_send.at[off],
            recv_sem=ag_recv.at[off],
            device_id={"gx": other(off)},
            device_id_type=pl.DeviceIdType.MESH,
        ).wait_recv()

    each(drain)
    packed_ref[...] = final_buf[...]


def unpack(state_ref, packed_ref, sg_ref, pg_ref, mg_ref, ug_ref):
    layers, features = mg_ref.shape[:2]
    sg_ref[...] = state_ref[...]
    for l in range(layers):
        base = l * 3 * features
        pg_ref[l, 0] = packed_ref[base : base + features, :features]
        pg_ref[l, 1] = packed_ref[base : base + features, features:]
        ug_ref[l] = packed_ref[base + features : base + 2 * features, :]
        mg_ref[l] = packed_ref[base + 2 * features : base + 3 * features, :features]


def local(size, *args):
    state, nb, _, face, mig = args[:5]
    pair, msg, upd = args[8], args[10], args[11]
    steps, slots, parts = nb.shape
    layers, features = msg.shape[:2]
    halo = face.shape[2]
    joint = parts + 2 * halo
    groups = slots // GROUP
    wide = GROUP * parts
    trades = 2 * steps * layers + 2 * (steps - 1)
    tiles = layers * 3 * features // 8
    chunk = -(-tiles // size) * 8
    rows = chunk * size
    vmem = pl.BlockSpec(memory_space=pltpu.VMEM)
    args = list(args)
    args[6] = jnp.transpose(args[6], (1, 0, 2))
    args[7] = args[7].T
    args[9] = jnp.transpose(args[9], (0, 2, 1))
    grads = pl.pallas_call(
        partial(kernel, size, chunk),
        out_shape=(
            jax.ShapeDtypeStruct(state.shape, F32),
            jax.ShapeDtypeStruct((rows, 128), F32),
        ),
        in_specs=[vmem] * len(args),
        out_specs=(vmem,) * 2,
        scratch_shapes=[
            pltpu.VMEM((steps, groups, joint, wide), BF16),
            pltpu.VMEM((steps, groups, 8, wide), F32),
            pltpu.VMEM((steps, groups, 8, wide), F32),
            pltpu.VMEM((steps, groups, 8, wide), F32),
            pltpu.VMEM((steps, layers, groups, 2 * features, wide), BF16),
            pltpu.VMEM((steps, layers, groups, features, wide), F32),
            pltpu.VMEM((steps, layers, groups, features, wide), F32),
            pltpu.VMEM((groups, 2 * features + 16, wide), BF16),
            pltpu.VMEM((groups, 2 * features, wide), BF16),
            pltpu.VMEM((steps, parts, 2 * halo), BF16),
            pltpu.VMEM((steps, 24, parts), F32),
            pltpu.VMEM((trades, 2, features + 8, halo), F32),
            pltpu.VMEM((trades, 2, features + 8, halo), F32),
            pltpu.VMEM((rows, 128), F32),
            pltpu.VMEM((size, chunk, 128), F32),
            pltpu.VMEM((rows, 128), F32),
            pltpu.SemaphoreType.DMA((trades, 2)),
            pltpu.SemaphoreType.DMA((trades, 2)),
            pltpu.SemaphoreType.DMA((size,)),
            pltpu.SemaphoreType.DMA((size,)),
            pltpu.SemaphoreType.DMA((size,)),
            pltpu.SemaphoreType.DMA((size,)),
        ],
        compiler_params=pltpu.CompilerParams(
            collective_id=0, has_side_effects=True, vmem_limit_bytes=56 * 1024 * 1024
        ),
    )(*args)
    return pl.pallas_call(
        unpack,
        out_shape=tuple(
            jax.ShapeDtypeStruct(a.shape, F32) for a in (state, pair, msg, upd)
        ),
        in_specs=[vmem] * 2,
        out_specs=(vmem,) * 4,
    )(*grads)


def solution(mesh):
    block = ("groups", "gx")
    in_specs = (
        P(None, block),
        P(None, None, block),
        P(None, None, block),
        P(None, None, block),
        P(None, None, block),
        P(None, block),
        P(None, None, block),
    ) + (P(),) * 7
    out_specs = (
        P(None, block),
        P("groups", None, None, None),
        P("groups", None, None),
        P("groups", None, None),
    )
    return jax.shard_map(
        partial(local, mesh.shape["gx"]),
        mesh=mesh,
        in_specs=in_specs,
        out_specs=out_specs,
        check_vma=False,
    )
```

```python
from functools import partial
import math

import jax
import jax.numpy as jnp
from jax import lax
from jax.experimental import pallas as pl
from jax.experimental.pallas import tpu as pltpu
from jax.sharding import PartitionSpec as P

HIGHEST = lax.Precision.HIGHEST
TIME_STEP = 0.5
EPSILON = 1e-05
F32 = jnp.float32
BF16 = jnp.bfloat16
GROUP = 12


def dot_nt(a, b, precision=HIGHEST):
    return lax.dot_general(
        a, b, (((1,), (1,)), ((), ())), precision=precision, preferred_element_type=F32
    )


def split(x):
    high = x.astype(BF16)
    low = (x - high.astype(F32)).astype(BF16)
    return high, low


def split_rows(x):
    high, low = split(x)
    return jnp.concatenate([high, low], axis=0)


def wide_weight(w):
    high = w.astype(BF16).astype(F32)
    return jnp.concatenate([high, high, w - high], axis=1).astype(BF16)


def dot(a, b):
    high, low = split(b)
    pieces = jnp.concatenate([high, low, high], axis=0)
    return jnp.dot(wide_weight(a), pieces, preferred_element_type=F32)


def hot(values, rows, start=0):
    count = lax.broadcasted_iota(jnp.int32, (rows, values.shape[1]), 0) + start
    return jnp.where(count == values, 1.0, 0.0).astype(BF16)


def kernel(
    size,
    chunk,
    state_ref,
    nb_ref,
    mask_ref,
    face_ref,
    mig_ref,
    order_ref,
    loss_ref,
    enc_ref,
    pair_ref,
    geo_ref,
    msg_ref,
    upd_ref,
    gain_ref,
    dec_ref,
    sg_ref,
    packed_ref,
    oh_ref,
    mrow_ref,
    q_ref,
    r_ref,
    act_ref,
    slope_ref,
    mslope_ref,
    piece_ref,
    message_ref,
    faces_ref,
    pv_ref,
    sbuf,
    rbuf,
    gbuf,
    gather_buf,
    final_buf,
    send_sem,
    recv_sem,
    rs_send,
    rs_recv,
    ag_send,
    ag_recv,
):
    steps, slots, parts = nb_ref.shape
    layers, features = gain_ref.shape
    halo = face_ref.shape[2]
    moved = mig_ref.shape[2]
    joint = parts + 2 * halo
    wide = GROUP * parts
    groups = slots // GROUP
    block = 3 * features
    me = lax.axis_index("gx")

    def other(off):
        return lax.rem(me + off, size)

    barrier = pltpu.get_barrier_semaphore()

    def greet(off, carry):
        pl.semaphore_signal(
            barrier, inc=1, device_id={"gx": other(off)}, device_id_type=pl.DeviceIdType.MESH
        )
        return carry

    lax.fori_loop(1, size, greet, 0)

    for s in range(steps):

        def build(c, carry):
            for k in range(GROUP):
                row = c * GROUP + k
                lanes = slice(k * parts, (k + 1) * parts)
                oh_ref[s, c, :, lanes] = hot(nb_ref[s, pl.ds(row, 1), :], joint)
                mrow_ref[s, c, 0:1, lanes] = mask_ref[s, pl.ds(row, 1), :].astype(F32) * (
                    1.0 / slots
                )
            return carry

        lax.fori_loop(0, groups, build, 0)
        for d in range(2):
            faces_ref[s, :, d * halo : (d + 1) * halo] = hot(face_ref[s, d : d + 1, :], parts)

    pv_ref[...] = jnp.zeros_like(pv_ref)
    q_ref[...] = jnp.zeros_like(q_ref)
    sbuf[...] = jnp.zeros_like(sbuf)
    gbuf[...] = jnp.zeros_like(gbuf)

    @pl.when(me == 0)
    def _():
        rbuf[:, 0] = jnp.zeros(rbuf.shape[:1] + rbuf.shape[2:], F32)

    @pl.when(me == size - 1)
    def _():
        rbuf[:, 1] = jnp.zeros(rbuf.shape[:1] + rbuf.shape[2:], F32)

    pl.semaphore_wait(barrier, size - 1)

    def copies(x):
        up = pltpu.make_async_remote_copy(
            src_ref=sbuf.at[x, 0],
            dst_ref=rbuf.at[x, 0],
            send_sem=send_sem.at[x, 0],
            recv_sem=recv_sem.at[x, 0],
            device_id={"gx": me + 1},
            device_id_type=pl.DeviceIdType.MESH,
        )
        down = pltpu.make_async_remote_copy(
            src_ref=sbuf.at[x, 1],
            dst_ref=rbuf.at[x, 1],
            send_sem=send_sem.at[x, 1],
            recv_sem=recv_sem.at[x, 1],
            device_id={"gx": me - 1},
            device_id_type=pl.DeviceIdType.MESH,
        )
        return up, down

    def start(x):
        up, down = copies(x)
        pl.when(me < size - 1)(up.start)
        pl.when(me > 0)(down.start)

    def finish(x):
        up, down = copies(x)

        @pl.when(me > 0)
        def _():
            down.wait_send()
            up.wait_recv()

        @pl.when(me < size - 1)
        def _():
            up.wait_send()
            down.wait_recv()

    eye = jnp.where(
        lax.broadcasted_iota(jnp.int32, (features, features), 0)
        == lax.broadcasted_iota(jnp.int32, (features, features), 1),
        1.0,
        0.0,
    )

    def turn(rows):
        return dot_nt(eye, rows)

    encoder = turn(enc_ref[...])
    geometry = [turn(geo_ref[l]) for l in range(layers)]
    dec_t = turn(dec_ref[...])
    gain_t = turn(gain_ref[...])

    def spread_rows(columns, rows):
        return sum(columns[:, c : c + 1] * rows[c] for c in range(3))

    def fold_rows(columns, array):
        return [
            jnp.sum(columns[:, c : c + 1] * array, axis=0, keepdims=True) for c in range(3)
        ]

    def tiled(x):
        return jnp.concatenate([x] * GROUP, axis=1)

    def slot_sum(x):
        return sum(x[:, k * parts : (k + 1) * parts] for k in range(GROUP))

    order = order_ref[0:1, :]
    order_own = hot(order, parts)
    low_code = jnp.where(order >= parts + moved, order - parts - moved + halo, order - parts)
    order_halo = hot(low_code, 2 * halo)
    going = [hot(mig_ref[0, d : d + 1, :], parts) for d in range(2)]

    def hot_dot(x, selector):
        rows = x.shape[0]
        pair = jnp.dot(split_rows(x), selector, preferred_element_type=F32)
        return pair[:rows] + pair[rows:]

    def hot_dot_nt(x, selector):
        rows = x.shape[0]
        pair = dot_nt(split_rows(x), selector, None)
        return pair[:rows] + pair[rows:]

    places = [state_ref[c : c + 1, :] for c in range(3)]
    speeds = [state_ref[c + 3 : c + 4, :] for c in range(3)]
    history = {}
    x_id = 0
    for s in range(steps):
        for c in range(3):
            pv_ref[s, c : c + 1, :] = places[c]
        own_places = pv_ref[s, 0:8]
        latent = spread_rows(encoder, speeds)
        for l in range(layers):
            geo = geometry[l]
            table = dot(pair_ref[l, 1], latent) + spread_rows(geo, places)
            first = l == 0
            leaving = jnp.concatenate([table, own_places], axis=0) if first else table
            sent = hot_dot(leaving, faces_ref[s])
            count = leaving.shape[0]
            sbuf[x_id, 0, :count] = sent[:, :halo]
            sbuf[x_id, 1, :count] = sent[:, halo:]
            start(x_id)
            own = dot(pair_ref[l, 0], latent) - spread_rows(geo, places)
            base_update = dot(upd_ref[l, :, :features], latent)
            weight = wide_weight(msg_ref[l])
            own_wide = tiled(own)
            places_wide = tiled(own_places)
            geo_r = geo[:, 3:4]

            def cut(values, spots):
                pieces = split_rows(values)
                if spots is None:
                    return pieces
                high = spots.astype(BF16).astype(F32)
                rest = jnp.concatenate([high, spots - high], axis=0)
                return jnp.concatenate([pieces, rest.astype(BF16)], axis=0)

            def merge(taken):
                at = 2 * features
                values = taken[:features] + taken[features:at]
                return values, (taken[at : at + 8] + taken[at + 8 : at + 16] if first else None)

            near_pieces = cut(table, own_places if first else None)

            def near_edges(c, carry):
                senders, offsets = merge(
                    jnp.dot(near_pieces, oh_ref[s, c, :parts], preferred_element_type=F32)
                )
                slope_ref[s, l, c] = own_wide + senders
                if first:
                    q_ref[s, c] = offsets - places_wide
                return carry

            lax.fori_loop(0, groups, near_edges, 0)
            finish(x_id)
            arrived = jnp.concatenate([rbuf[x_id, 0], rbuf[x_id, 1]], axis=1)
            far_pieces = cut(arrived[:features], arrived[features:] if first else None)
            x_id += 1

            def edges(c, total):
                senders, offsets = merge(
                    jnp.dot(far_pieces, oh_ref[s, c, parts:], preferred_element_type=F32)
                )
                if first:
                    offsets = offsets + q_ref[s, c]
                    squared = jnp.sum(offsets * offsets, axis=0, keepdims=True) + 1.0
                    distance = jnp.sqrt(squared)
                    r_ref[s, c, 0:1, :] = distance
                    q_ref[s, c] = offsets / distance
                else:
                    distance = r_ref[s, c, 0:1, :]
                pre = slope_ref[s, l, c] + senders + geo_r * distance
                gate = 0.5 * jnp.tanh(0.5 * pre) + 0.5
                hidden = pre * gate
                slope_ref[s, l, c] = gate + hidden - hidden * gate
                both = split_rows(hidden)
                act_ref[s, l, c] = both
                pre2 = jnp.dot(
                    weight,
                    jnp.concatenate([both, both[:features]], axis=0),
                    preferred_element_type=F32,
                )
                gate2 = 0.5 * jnp.tanh(0.5 * pre2) + 0.5
                message = pre2 * gate2
                scale = mrow_ref[s, c, 0:1, :]
                mslope_ref[s, l, c] = (gate2 + message - message * gate2) * scale
                return total + slot_sum(message * scale)

            collected = lax.fori_loop(0, groups, edges, jnp.zeros((features, parts), F32))
            update = base_update + dot(upd_ref[l, :, features:], collected)
            centred = update - jnp.mean(update, axis=0, keepdims=True)
            spread = lax.rsqrt(jnp.mean(centred * centred, axis=0, keepdims=True) + EPSILON)
            normed = centred * spread
            history[s, l] = (latent, collected, normed, spread)
            latent = latent + gain_t[:, l : l + 1] * normed
        gained = fold_rows(dec_t, latent)
        speeds = [speeds[c] + TIME_STEP * gained[c] for c in range(3)]
        places = [places[c] + TIME_STEP * speeds[c] for c in range(3)]
        if s + 1 < steps:
            for c in range(3):
                pv_ref[s, 8 + c : 9 + c, :] = places[c]
                pv_ref[s, 16 + c : 17 + c, :] = speeds[c]
            advanced = pv_ref[s, 8:24]
            for d in range(2):
                sbuf[x_id, d, :16, :moved] = hot_dot(advanced, going[d])
            start(x_id)
            kept = hot_dot(advanced, order_own)
            finish(x_id)
            arrived = jnp.concatenate([rbuf[x_id, 0, :16], rbuf[x_id, 1, :16]], axis=1)
            pv_ref[s, 8:24] = kept + hot_dot(arrived, order_halo)
            x_id += 1
            places = [pv_ref[s, 8 + c : 9 + c, :] for c in range(3)]
            speeds = [pv_ref[s, 16 + c : 17 + c, :] for c in range(3)]

    carried = [None] * 6
    for s in reversed(range(steps)):
        grad_out = [loss_ref[c, s : s + 1, :] for c in range(6)]
        if carried[0] is not None:
            grad_out = [a + b for a, b in zip(grad_out, carried)]
        grad_places = grad_out[:3]
        grad_speeds = [grad_out[3 + c] + TIME_STEP * grad_out[c] for c in range(3)]
        grad_latent = spread_rows(dec_t, [TIME_STEP * g for g in grad_speeds])
        far_total = jnp.zeros((8, 2 * halo), F32)
        near_total = jnp.zeros((8, parts), F32)
        for l in reversed(range(layers)):
            latent, collected, normed, spread = history[s, l]
            geo = geometry[l]
            geo_r = geo[:, 3:4]
            g_norm = gain_t[:, l : l + 1] * grad_latent
            g_update = spread * (
                g_norm
                - jnp.mean(g_norm, axis=0, keepdims=True)
                - normed * jnp.mean(g_norm * normed, axis=0, keepdims=True)
            )
            upd_collected_t = upd_ref[l, :, features:].T
            g_wide = tiled(dot(upd_collected_t, g_update))
            weight_t = wide_weight(msg_ref[l].T)

            def back(c, carry):
                spread_sum, own_sum, near_sum = carry
                g_pre2 = g_wide * mslope_ref[s, l, c]
                both = split_rows(g_pre2)
                message_ref[c] = both
                g_hidden = jnp.dot(
                    weight_t,
                    jnp.concatenate([both, both[:features]], axis=0),
                    preferred_element_type=F32,
                )
                g_pre = g_hidden * slope_ref[s, l, c]
                g_distance = jnp.sum(geo_r * g_pre, axis=0, keepdims=True)
                g_offset = q_ref[s, c] * g_distance
                offset_high = g_offset.astype(BF16).astype(F32)
                offset_pieces = jnp.concatenate([offset_high, g_offset - offset_high], axis=0)
                pieces = jnp.concatenate([split_rows(g_pre), offset_pieces.astype(BF16)], axis=0)
                piece_ref[c] = pieces
                spread_sum = spread_sum + dot_nt(pieces, oh_ref[s, c, parts:], None)
                return (
                    spread_sum,
                    own_sum + slot_sum(g_pre),
                    near_sum + slot_sum(g_offset),
                )

            spread_sum, own_sum, near_sum = lax.fori_loop(
                0,
                groups,
                back,
                (
                    jnp.zeros((2 * features + 16, 2 * halo), F32),
                    jnp.zeros((features, parts), F32),
                    jnp.zeros((8, parts), F32),
                ),
            )
            at = 2 * features
            g_far = spread_sum[:features] + spread_sum[features:at]
            far_total = far_total + spread_sum[at : at + 8] + spread_sum[at + 8 : at + 16]
            sbuf[x_id, 1, :features] = g_far[:, :halo]
            sbuf[x_id, 0, :features] = g_far[:, halo:]
            if l == 0:
                sbuf[x_id, 1, features:] = far_total[:, :halo]
                sbuf[x_id, 0, features:] = far_total[:, halo:]
            start(x_id)

            def back_own(c, carry):
                spread_sum, weight_sum = carry
                return (
                    spread_sum + dot_nt(piece_ref[c], oh_ref[s, c, :parts], None),
                    weight_sum + dot_nt(message_ref[c], act_ref[s, l, c], None),
                )

            spread_sum, weight_sum = lax.fori_loop(
                0,
                groups,
                back_own,
                (
                    jnp.zeros((2 * features + 16, parts), F32),
                    jnp.zeros((2 * features, 2 * features), F32),
                ),
            )
            g_table = spread_sum[:features] + spread_sum[features:at]
            near_total = near_total + spread_sum[at : at + 8] + spread_sum[at + 8 : at + 16]
            near_total = near_total - near_sum
            base = l * block
            gbuf[base + features : base + 2 * features, :] += dot_nt(
                g_update, jnp.concatenate([latent, collected], axis=0)
            )
            gbuf[base + 2 * features : base + block, :features] += (
                weight_sum[:features, :features]
                + weight_sum[features:, :features]
                + weight_sum[:features, features:]
                + weight_sum[features:, features:]
            )
            grad_latent = (
                grad_latent
                + dot(upd_ref[l, :, :features].T, g_update)
                + dot(pair_ref[l, 0].T, own_sum)
            )
            finish(x_id)
            returned = jnp.concatenate([rbuf[x_id, 1], rbuf[x_id, 0]], axis=1)
            if l > 0:
                returned = returned[:features]
            x_id += 1
            settled = hot_dot_nt(returned, faces_ref[s])
            g_table = g_table + settled[:features]
            grad_latent = grad_latent + dot(pair_ref[l, 1].T, g_table)
            grad_places = [
                a + b for a, b in zip(grad_places, fold_rows(geo, g_table - own_sum))
            ]
            if l == 0:
                near = near_total + settled[features:]
                grad_places = [grad_places[c] + near[c : c + 1] for c in range(3)]
            gbuf[base : base + features, :] += jnp.concatenate(
                [dot_nt(own_sum, latent), dot_nt(g_table, latent)], axis=1
            )
        grad_speeds = [
            a + b for a, b in zip(grad_speeds, fold_rows(encoder, grad_latent))
        ]
        if s > 0:
            for c in range(3):
                pv_ref[s, 8 + c : 9 + c, :] = grad_places[c]
                pv_ref[s, 16 + c : 17 + c, :] = grad_speeds[c]
            current = pv_ref[s, 8:24]
            handed = hot_dot_nt(current, order_halo)
            sbuf[x_id, 1, :16] = handed[:, :halo]
            sbuf[x_id, 0, :16] = handed[:, halo:]
            start(x_id)
            kept = hot_dot_nt(current, order_own)
            finish(x_id)
            pv_ref[s, 8:24] = (
                kept
                + hot_dot_nt(rbuf[x_id, 1, :16, :moved], going[0])
                + hot_dot_nt(rbuf[x_id, 0, :16, :moved], going[1])
            )
            x_id += 1
            carried = [pv_ref[s, 8 + c : 9 + c, :] for c in range(3)]
            carried += [pv_ref[s, 16 + c : 17 + c, :] for c in range(3)]
        else:
            for c in range(3):
                sg_ref[c : c + 1, :] = grad_places[c]
                sg_ref[3 + c : 4 + c, :] = grad_speeds[c]

    def rows_of(index):
        return pl.ds(pl.multiple_of(index * chunk, 8), chunk)

    def scatter_copy(off):
        return pltpu.make_async_remote_copy(
            src_ref=gbuf.at[rows_of(other(off))],
            dst_ref=gather_buf.at[off],
            send_sem=rs_send.at[off],
            recv_sem=rs_recv.at[off],
            device_id={"gx": other(off)},
            device_id_type=pl.DeviceIdType.MESH,
        )

    def gather_copy(off):
        return pltpu.make_async_remote_copy(
            src_ref=final_buf.at[rows_of(me)],
            dst_ref=final_buf.at[rows_of(me)],
            send_sem=ag_send.at[off],
            recv_sem=ag_recv.at[off],
            device_id={"gx": other(off)},
            device_id_type=pl.DeviceIdType.MESH,
        )

    def each(act):
        def body(off, carry):
            act(off)
            return carry

        lax.fori_loop(1, size, body, 0)

    each(lambda off: scatter_copy(off).start())

    def add(off, total):
        scatter_copy(off).wait_recv()
        return total + gather_buf[off]

    total = lax.fori_loop(1, size, add, gbuf[rows_of(me), :])
    final_buf[rows_of(me), :] = total * (1.0 / math.sqrt(parts * size))
    each(lambda off: gather_copy(off).start())

    def drain(off):
        scatter_copy(off).wait_send()
        gather_copy(off).wait_send()
        source = lax.rem(me - off + size, size)
        pltpu.make_async_remote_copy(
            src_ref=final_buf.at[rows_of(source)],
            dst_ref=final_buf.at[rows_of(source)],
            send_sem=ag_send.at[off],
            recv_sem=ag_recv.at[off],
            device_id={"gx": other(off)},
            device_id_type=pl.DeviceIdType.MESH,
        ).wait_recv()

    each(drain)
    packed_ref[...] = final_buf[...]


def unpack(state_ref, packed_ref, sg_ref, pg_ref, mg_ref, ug_ref):
    layers, features = mg_ref.shape[:2]
    sg_ref[...] = state_ref[...]
    for l in range(layers):
        base = l * 3 * features
        pg_ref[l, 0] = packed_ref[base : base + features, :features]
        pg_ref[l, 1] = packed_ref[base : base + features, features:]
        ug_ref[l] = packed_ref[base + features : base + 2 * features, :]
        mg_ref[l] = packed_ref[base + 2 * features : base + 3 * features, :features]


def local(size, *args):
    state, nb, _, face, mig = args[:5]
    pair, msg, upd = args[8], args[10], args[11]
    steps, slots, parts = nb.shape
    layers, features = msg.shape[:2]
    halo = face.shape[2]
    joint = parts + 2 * halo
    groups = slots // GROUP
    wide = GROUP * parts
    trades = 2 * steps * layers + 2 * (steps - 1)
    tiles = layers * 3 * features // 8
    chunk = -(-tiles // size) * 8
    rows = chunk * size
    vmem = pl.BlockSpec(memory_space=pltpu.VMEM)
    args = list(args)
    args[6] = jnp.transpose(args[6], (1, 0, 2))
    args[7] = args[7].T
    args[9] = jnp.transpose(args[9], (0, 2, 1))
    grads = pl.pallas_call(
        partial(kernel, size, chunk),
        out_shape=(
            jax.ShapeDtypeStruct(state.shape, F32),
            jax.ShapeDtypeStruct((rows, 128), F32),
        ),
        in_specs=[vmem] * len(args),
        out_specs=(vmem,) * 2,
        scratch_shapes=[
            pltpu.VMEM((steps, groups, joint, wide), BF16),
            pltpu.VMEM((steps, groups, 8, wide), F32),
            pltpu.VMEM((steps, groups, 8, wide), F32),
            pltpu.VMEM((steps, groups, 8, wide), F32),
            pltpu.VMEM((steps, layers, groups, 2 * features, wide), BF16),
            pltpu.VMEM((steps, layers, groups, features, wide), F32),
            pltpu.VMEM((steps, layers, groups, features, wide), F32),
            pltpu.VMEM((groups, 2 * features + 16, wide), BF16),
            pltpu.VMEM((groups, 2 * features, wide), BF16),
            pltpu.VMEM((steps, parts, 2 * halo), BF16),
            pltpu.VMEM((steps, 24, parts), F32),
            pltpu.VMEM((trades, 2, features + 8, halo), F32),
            pltpu.VMEM((trades, 2, features + 8, halo), F32),
            pltpu.VMEM((rows, 128), F32),
            pltpu.VMEM((size, chunk, 128), F32),
            pltpu.VMEM((rows, 128), F32),
            pltpu.SemaphoreType.DMA((trades, 2)),
            pltpu.SemaphoreType.DMA((trades, 2)),
            pltpu.SemaphoreType.DMA((size,)),
            pltpu.SemaphoreType.DMA((size,)),
            pltpu.SemaphoreType.DMA((size,)),
            pltpu.SemaphoreType.DMA((size,)),
        ],
        compiler_params=pltpu.CompilerParams(
            collective_id=0, has_side_effects=True, vmem_limit_bytes=56 * 1024 * 1024
        ),
    )(*args)
    return pl.pallas_call(
        unpack,
        out_shape=tuple(
            jax.ShapeDtypeStruct(a.shape, F32) for a in (state, pair, msg, upd)
        ),
        in_specs=[vmem] * 2,
        out_specs=(vmem,) * 4,
    )(*grads)


def solution(mesh):
    block = ("groups", "gx")
    in_specs = (
        P(None, block),
        P(None, None, block),
        P(None, None, block),
        P(None, None, block),
        P(None, None, block),
        P(None, block),
        P(None, None, block),
    ) + (P(),) * 7
    out_specs = (
        P(None, block),
        P("groups", None, None, None),
        P("groups", None, None),
        P("groups", None, None),
    )
    return jax.shard_map(
        partial(local, mesh.shape["gx"]),
        mesh=mesh,
        in_specs=in_specs,
        out_specs=out_specs,
        check_vma=False,
    )
```
